32 devices in a mesh: half: 2 (over core), rows: 16 (over z, y, x).
Axes of the slice: x: 2, y: 2, z: 4, core: 2. Of those that a mesh axis runs over, the one named last changes fastest.
Arguments:
- factors: float32 [2, 16384, 256], P('half', 'rows'), may hold values from -8 to 8
- coefficients: float32 [256, 256], replicated, may hold values from -1 to 9
- density: float32 [16384], P('rows'), may hold values from 0.25 to 4
Outputs:
- new_factors: float32 [2, 16384, 256], P('half', 'rows')
- new_coefficients: float32 [256, 256], P('half')
The draws below stay inside these ranges and needn't reach their ends.
All inputs are finite; a program needn't handle non-finite values.
Results may differ from the reference program's by a relative error of at most 0.0001.
Values sent between devices are 32-bit elements; how exact they have to be, the bound alone decides.
A program may use at most 128 MiB of HBM per device.

```python
import jax
import jax.numpy as jnp
from jax import lax

R = 256
NY = 32
NZ = 32
VGRID = 64
NR = 16384
NX = 16


def density_values(key):
    return jnp.exp(jax.random.uniform(jax.random.fold_in(key, 37), (NR,), jnp.float32, -1.3862944, 1.3862944))


def draw_density(key, part):
    return density_values(key)


def draw_factors(key, part):
    first_key, second_key = jax.random.split(jax.random.fold_in(key, 11))
    space_factor = jnp.clip(jax.random.normal(first_key, (NR, R), jnp.float32), -6.0, 6.0)
    velocity_factor = jnp.clip(jax.random.normal(second_key, (NR, R), jnp.float32), -6.0, 6.0)
    cell_density = density_values(key)
    density_column = cell_density / jnp.sqrt(jnp.mean(cell_density * cell_density))
    space_factor = space_factor.at[:, 0].set(density_column + 0.4 * space_factor[:, 0])
    last_points = NR // (VGRID * VGRID)
    row_index = jnp.arange(NR, dtype=jnp.int32)
    third_index = row_index % last_points
    second = row_index // last_points % VGRID
    first_index = row_index // (last_points * VGRID)
    speeds = jnp.stack([-1.0 + (2 * first_index + 1).astype(jnp.float32) / VGRID, -1.0 + (2 * second + 1).astype(jnp.float32) / VGRID, -1.0 + (2 * third_index + 1).astype(jnp.float32) / last_points])
    maxwell = jnp.exp(-2.0 * jnp.sum(speeds * speeds, axis=0))
    column = maxwell / jnp.sqrt(jnp.mean(maxwell * maxwell))
    velocity_factor = velocity_factor.at[:, 0].set(column + 0.4 * velocity_factor[:, 0])
    return jnp.stack([space_factor, velocity_factor])


def draw_coefficients(key, part):
    first_key, second_key = jax.random.split(jax.random.fold_in(key, 23))
    diagonal = jnp.exp(jax.random.uniform(first_key, (R,), jnp.float32, 0.6931472, 2.0794415))
    noise = jnp.clip(jax.random.normal(second_key, (R, R), jnp.float32), -6.0, 6.0)
    return jnp.diag(diagonal) + 0.5 / jnp.sqrt(float(R)) * noise


def setup_inputs(seed: int = 0) -> dict:
    keys = jax.random.split(jax.random.key(seed), 4)
    return {
        "factors": draw_factors(jax.random.fold_in(keys[3], 71), 0),
        "coefficients": draw_coefficients(jax.random.fold_in(keys[3], 71), 0),
        "density": draw_density(jax.random.fold_in(keys[3], 71), 0),
    }


time_step = 0.2
relax_time = 0.5

def project(left, right, total_rows):
    return lax.dot_general(left.astype(jnp.float32), right.astype(jnp.float32), (((0,), (0,)), ((), ())), precision=lax.Precision.HIGHEST, preferred_element_type=jnp.float32) / total_rows

def matmul(left, right):
    return jnp.dot(left.astype(jnp.float32), right.astype(jnp.float32), precision=lax.Precision.HIGHEST, preferred_element_type=jnp.float32)

def velocity_grid(start, row_count, total_rows):
    last_points = total_rows // (VGRID * VGRID)
    row_index = start + jnp.arange(row_count, dtype=jnp.int32)
    third_index = row_index % last_points
    second = row_index // last_points % VGRID
    first_index = row_index // (last_points * VGRID)
    speeds = jnp.stack([-1.0 + (2 * first_index + 1).astype(jnp.float32) / VGRID, -1.0 + (2 * second + 1).astype(jnp.float32) / VGRID, -1.0 + (2 * third_index + 1).astype(jnp.float32) / last_points])
    maxwell = jnp.exp(-2.0 * jnp.sum(speeds * speeds, axis=0))
    return (speeds, maxwell)

def grid_slopes(values):
    width = values.shape[3]
    slopes = []
    for axis_index in range(3):
        minus_part = values - jnp.roll(values, 1, axis_index)
        plus_part = jnp.roll(values, -1, axis_index) - values
        slopes.append((minus_part.reshape(-1, width), plus_part.reshape(-1, width)))
    return slopes

def space_moments(local_factor, slopes, density, total_rows):
    matrices = [project(local_factor, pair[0], total_rows) for pair in slopes]
    matrices = matrices + [project(local_factor, pair[1], total_rows) for pair in slopes]
    return (jnp.stack(matrices), project(local_factor, density[:, None], total_rows)[:, 0])

def velocity_moments(local_factor, speeds, maxwell, total_rows):
    plus_speed = jnp.maximum(speeds, 0.0)
    minus_speed = jnp.minimum(speeds, 0.0)
    matrices = [project(local_factor, plus_speed[k][:, None] * local_factor, total_rows) for k in range(3)]
    matrices = matrices + [project(local_factor, minus_speed[k][:, None] * local_factor, total_rows) for k in range(3)]
    return (jnp.stack(matrices), project(local_factor, maxwell[:, None], total_rows)[:, 0])

def space_update(local_factor, slopes, coefficients, velocity_set, density):
    matrices, vector = velocity_set
    product = matmul(local_factor, coefficients)
    transport = jnp.zeros_like(product)
    for direction in range(3):
        transport = transport + matmul(slopes[direction][0], matmul(coefficients, matrices[direction]))
        transport = transport + matmul(slopes[direction][1], matmul(coefficients, matrices[3 + direction]))
    return product - time_step * transport + time_step / relax_time * (density[:, None] * vector[None, :] - product)

def velocity_update(local_factor, speeds, maxwell, coefficients, space_set):
    matrices, vector = space_set
    plus_speed = jnp.maximum(speeds, 0.0)
    minus_speed = jnp.minimum(speeds, 0.0)
    product = matmul(local_factor, coefficients.T)
    transport = jnp.zeros_like(product)
    for direction in range(3):
        transport = transport + plus_speed[direction][:, None] * matmul(product, matrices[direction].T)
        transport = transport + minus_speed[direction][:, None] * matmul(product, matrices[3 + direction].T)
    return product - time_step * transport + time_step / relax_time * (maxwell[:, None] * vector[None, :] - product)

def from_lower(values, lower_factor):
    identity = jnp.eye(lower_factor.shape[0], dtype=jnp.float32)
    inverse = jax.scipy.linalg.solve_triangular(lower_factor, identity, lower=True)
    return matmul(values, inverse.T)

def coefficient_step(coefficients, space_set, velocity_set):
    space_mats, space_vector = space_set
    velocity_mats, velocity_vector = velocity_set
    galerkin = matmul(matmul(space_mats[0], coefficients), velocity_mats[0].T)
    transport = jnp.zeros_like(galerkin)
    for direction in range(3):
        transport = transport + matmul(matmul(space_mats[1 + direction], galerkin), velocity_mats[1 + direction])
        transport = transport + matmul(matmul(space_mats[4 + direction], galerkin), velocity_mats[4 + direction])
    return galerkin - time_step * transport + time_step / relax_time * (space_vector[:, None] * velocity_vector[None, :] - galerkin)

def reference(factors, coefficients, density):
    space_factor = factors[0]
    velocity_factor = factors[1]
    speeds, maxwell = velocity_grid(0, NR, NR)
    slopes = grid_slopes(space_factor.reshape(NX, NY, NZ, R))
    space_set = space_moments(space_factor, slopes, density, NR)
    velocity_set = velocity_moments(velocity_factor, speeds, maxwell, NR)
    k_field = space_update(space_factor, slopes, coefficients, velocity_set, density)
    l_field = velocity_update(velocity_factor, speeds, maxwell, coefficients, space_set)
    space_basis = from_lower(k_field, jnp.linalg.cholesky(project(k_field, k_field, NR)))
    velocity_basis = from_lower(l_field, jnp.linalg.cholesky(project(l_field, l_field, NR)))
    new_slopes = grid_slopes(space_basis.reshape(NX, NY, NZ, R))
    space_mats, space_vector = space_moments(space_basis, new_slopes, density, NR)
    space_two = (jnp.concatenate([project(space_basis, space_factor, NR)[None], space_mats]), space_vector)
    velocity_mats, velocity_vector = velocity_moments(velocity_basis, speeds, maxwell, NR)
    velocity_two = (jnp.concatenate([project(velocity_basis, velocity_factor, NR)[None], velocity_mats]), velocity_vector)
    updated = coefficient_step(coefficients, space_two, velocity_two)
    return (jnp.stack([space_basis, velocity_basis]), updated)
```

```python
import functools

import jax
import jax.numpy as jnp
from jax import lax
from jax.experimental import pallas as pl
from jax.experimental.pallas import tpu as pltpu
from jax.sharding import PartitionSpec as P

NY = 32
NZ = 32
VGRID = 64

time_step = 0.2
relax_time = 0.5
relax = time_step / relax_time

MESH = pl.DeviceIdType.MESH
PREC = lax.Precision.HIGHEST


def project(left, right):
    return lax.dot_general(
        left,
        right,
        (((0,), (0,)), ((), ())),
        precision=PREC,
        preferred_element_type=jnp.float32,
    )


def matmul(left, right):
    return jnp.dot(left, right, precision=PREC, preferred_element_type=jnp.float32)


def matmul_t(left, right):
    return lax.dot_general(
        left,
        right,
        (((1,), (1,)), ((), ())),
        precision=PREC,
        preferred_element_type=jnp.float32,
    )


def share_kernel(n, inner, swap, p_ref, o_ref, acc, got_in, got_out, mine, full, *sems):
    (s_a, r_a, s_b, r_b, s_s, r_s, s_c, r_c, s_d, r_d) = sems
    outer = n // inner
    half = lax.axis_index("half")
    row = lax.axis_index("rows")
    b = lax.rem(row, inner)
    a = row // inner
    q = p_ref.shape[0] // n
    w = q * outer

    def in_peer(k):
        return lax.rem(b + k, inner)

    def out_peer(k):
        return lax.rem(a + k, outer)

    peers = [(half, a * inner + in_peer(k)) for k in range(1, inner)]
    peers += [(half, out_peer(k) * inner + b) for k in range(1, outer)]
    if swap:
        peers.append((1 - half, row))
    barrier = pltpu.get_barrier_semaphore()
    for peer in peers:
        pl.semaphore_signal(barrier, inc=1, device_id=peer, device_id_type=MESH)
    pl.semaphore_wait(barrier, len(peers))

    def remote(src, dst, send, recv, peer):
        copy = pltpu.make_async_remote_copy(
            src_ref=src,
            dst_ref=dst,
            send_sem=send,
            recv_sem=recv,
            device_id=peer,
            device_id_type=MESH,
        )
        copy.start()
        return copy

    copies = []
    for k in range(1, inner):
        t = in_peer(k)
        rows = pl.ds(pl.multiple_of(t * w, 8), w)
        copies.append(
            remote(p_ref.at[rows], got_in.at[k - 1], s_a.at[k - 1], r_a.at[k - 1], (half, a * inner + t))
        )
    for copy in copies:
        copy.wait()
    total = p_ref[pl.ds(pl.multiple_of(b * w, 8), w), :]
    for k in range(1, inner):
        total = total + got_in[k - 1]
    acc[...] = total

    copies = []
    for k in range(1, outer):
        t = out_peer(k)
        rows = pl.ds(pl.multiple_of(t * q, 8), q)
        copies.append(
            remote(acc.at[rows], got_out.at[k - 1], s_b.at[k - 1], r_b.at[k - 1], (half, t * inner + b))
        )
    for copy in copies:
        copy.wait()
    piece = acc[pl.ds(pl.multiple_of(a * q, 8), q), :]
    for k in range(1, outer):
        piece = piece + got_out[k - 1]
    spot = pl.ds(pl.multiple_of(b * w + a * q, 8), q)
    if swap:
        mine[...] = piece
        copy = remote(mine, full.at[spot], s_s.at[0], r_s.at[0], (1 - half, row))
        copy.wait()
    else:
        full[spot, :] = piece

    copies = []
    for k in range(1, outer):
        t = out_peer(k)
        copies.append(
            remote(full.at[spot], full.at[spot], s_c.at[k - 1], r_c.at[k - 1], (half, t * inner + b))
        )
    for copy in copies:
        copy.wait()
    wide = pl.ds(pl.multiple_of(b * w, 8), w)
    copies = []
    for k in range(1, inner):
        t = in_peer(k)
        copies.append(
            remote(full.at[wide], full.at[wide], s_d.at[k - 1], r_d.at[k - 1], (half, a * inner + t))
        )
    for copy in copies:
        copy.wait()
    o_ref[...] = full[...]


def share_rows(payload, swap, collective_id):
    n = lax.axis_size("rows")
    inner = 4 if n % 4 == 0 and n > 4 else 2
    outer = n // inner
    rows, cols = payload.shape
    q = rows // n
    dma = pltpu.SemaphoreType.DMA
    sems = []
    for count in (inner - 1, outer - 1, 1, outer - 1, inner - 1):
        sems += [dma((count,)), dma((count,))]
    f32 = jnp.float32
    return pl.pallas_call(
        functools.partial(share_kernel, n, inner, swap),
        out_shape=jax.ShapeDtypeStruct((rows, cols), f32),
        in_specs=[pl.BlockSpec(memory_space=pltpu.VMEM)],
        out_specs=pl.BlockSpec(memory_space=pltpu.VMEM),
        scratch_shapes=[
            pltpu.VMEM((q * outer, cols), f32),
            pltpu.VMEM((inner - 1, q * outer, cols), f32),
            pltpu.VMEM((outer - 1, q, cols), f32),
            pltpu.VMEM((q, cols), f32),
            pltpu.VMEM((rows, cols), f32),
        ]
        + sems,
        compiler_params=pltpu.CompilerParams(
            collective_id=collective_id, has_side_effects=True, vmem_limit_bytes=32 * 1024 * 1024
        ),
    )(payload)


def padded_rows(rows, n):
    unit = 8 * n
    return (rows + unit - 1) // unit * unit


def velocity_grid(start, row_count, total_rows):
    last_points = total_rows // (VGRID * VGRID)
    row_index = start + jnp.arange(row_count, dtype=jnp.int32)
    third_index = row_index % last_points
    second = row_index // last_points % VGRID
    first_index = row_index // (last_points * VGRID)
    speeds = jnp.stack(
        [
            -1.0 + (2 * first_index + 1).astype(jnp.float32) / VGRID,
            -1.0 + (2 * second + 1).astype(jnp.float32) / VGRID,
            -1.0 + (2 * third_index + 1).astype(jnp.float32) / last_points,
        ]
    )
    maxwell = jnp.exp(-2.0 * jnp.sum(speeds * speeds, axis=0))
    return (speeds, maxwell)


def neighbour_plane(plane, step):
    count = lax.axis_size("rows")
    pairs = [(i, (i + step) % count) for i in range(count)]
    return lax.ppermute(plane, ("half", "rows"), pairs)


def back_slopes(block, low):
    width = block.shape[3]
    shifted = jnp.concatenate([low, block[:-1]], axis=0)
    slopes = [block - shifted]
    for axis_index in (1, 2):
        slopes.append(block - jnp.roll(block, 1, axis_index))
    return [s.reshape(-1, width) for s in slopes]


def front_slopes(block, high):
    width = block.shape[3]
    shifted = jnp.concatenate([block[1:], high], axis=0)
    slopes = [shifted - block]
    for axis_index in (1, 2):
        slopes.append(jnp.roll(block, -1, axis_index) - block)
    return [s.reshape(-1, width) for s in slopes]


def pack_payload(blocks, extras, rows, total_rows):
    rank = blocks[0].shape[1]
    used = sum(block.shape[0] for block in blocks)
    extra = jnp.stack(extras)
    pad = jnp.zeros((rows - used - extra.shape[0], rank), jnp.float32)
    return jnp.concatenate(blocks + [extra, pad]) * (1.0 / total_rows)


def triangle(rank):
    i = lax.broadcasted_iota(jnp.int32, (rank, rank), 0)
    j = lax.broadcasted_iota(jnp.int32, (rank, rank), 1)
    return i, j


def pack_pair(plus, minus):
    i, j = triangle(plus.shape[0])
    return jnp.where(i >= j, plus, minus), jnp.sum(jnp.where(i == j, minus, 0.0), axis=0)


def unpack_pair(packed, minus_diagonal):
    i, j = triangle(packed.shape[0])
    flipped = packed.T
    plus = jnp.where(i >= j, packed, flipped)
    minus = jnp.where(i < j, packed, jnp.where(i == j, minus_diagonal[None, :], flipped))
    return plus, minus


def space_blocks(factor, slopes):
    return [project(factor, slope) for slope in slopes]


def velocity_blocks(factor, speeds):
    plus_speed = jnp.maximum(speeds, 0.0)
    minus_speed = jnp.minimum(speeds, 0.0)
    blocks, diagonals = [], []
    for k in range(3):
        block, diagonal = pack_pair(
            project(factor, plus_speed[k][:, None] * factor),
            project(factor, minus_speed[k][:, None] * factor),
        )
        blocks.append(block)
        diagonals.append(diagonal)
    return blocks, diagonals


def weighted(factor, weight):
    return project(weight[:, None], factor)[0]


def lower_inverse(gram):
    lower = jnp.linalg.cholesky(gram)
    identity = jnp.eye(lower.shape[0], dtype=jnp.float32)
    return jax.scipy.linalg.solve_triangular(lower, identity, lower=True)


def local(factors, coefficients, density):
    rank = factors.shape[2]
    rows_here = factors.shape[1]
    n = lax.axis_size("rows")
    total_rows = rows_here * n
    planes = rows_here // (NY * NZ)
    start = lax.axis_index("rows") * rows_here
    on_space = lax.axis_index("half") == 0
    factor = factors[0]
    speeds, maxwell = velocity_grid(start, rows_here, total_rows)
    block = factor.reshape(planes, NY, NZ, rank)
    low = neighbour_plane(block[-1:], 1)
    high = neighbour_plane(block[:1], -1)
    zero_row = jnp.zeros((rank,), jnp.float32)

    size_one = padded_rows(3 * rank + 4, n)

    def space_first():
        blocks = space_blocks(factor, back_slopes(block, low))
        extras = [weighted(factor, density), zero_row, zero_row, zero_row]
        return pack_payload(blocks, extras, size_one, total_rows)

    def velocity_first():
        blocks, diagonals = velocity_blocks(factor, speeds)
        extras = [weighted(factor, maxwell)] + diagonals
        return pack_payload(blocks, extras, size_one, total_rows)

    other = share_rows(lax.cond(on_space, space_first, velocity_first), True, 0)
    vector = other[3 * rank]

    def space_update():
        back = back_slopes(block, low)
        front = front_slopes(block, high)
        fresh = (1.0 - relax) * matmul(factor, coefficients)
        for k in range(3):
            plus, minus = unpack_pair(other[k * rank : (k + 1) * rank], other[3 * rank + 1 + k])
            fresh = fresh + matmul(back[k], matmul(coefficients * (-time_step), plus))
            fresh = fresh + matmul(front[k], matmul(coefficients * (-time_step), minus))
        return fresh + relax * (density[:, None] * vector[None, :])

    def velocity_update():
        plus_speed = jnp.maximum(speeds, 0.0) * (-time_step)
        minus_speed = jnp.minimum(speeds, 0.0) * time_step
        product = matmul_t(factor, coefficients)
        fresh = (1.0 - relax) * product
        for k in range(3):
            moment = other[k * rank : (k + 1) * rank]
            fresh = fresh + plus_speed[k][:, None] * matmul_t(product, moment)
            fresh = fresh + minus_speed[k][:, None] * matmul(product, moment)
        return fresh + relax * (maxwell[:, None] * vector[None, :])

    fresh = lax.cond(on_space, space_update, velocity_update)
    fresh_block = fresh.reshape(planes, NY, NZ, rank)
    fresh_low = neighbour_plane(fresh_block[-1:], 1)
    gram = project(fresh, fresh)
    cross = project(fresh, factor)

    size_two = padded_rows(5 * rank + 4, n)

    def space_second():
        blocks = space_blocks(fresh, back_slopes(fresh_block, fresh_low))
        extras = [weighted(fresh, density), zero_row, zero_row, zero_row]
        return pack_payload([gram, cross] + blocks, extras, size_two, total_rows)

    def velocity_second():
        blocks, diagonals = velocity_blocks(fresh, speeds)
        extras = [weighted(fresh, maxwell)] + diagonals
        return pack_payload([gram, cross] + blocks, extras, size_two, total_rows)

    sums = share_rows(lax.cond(on_space, space_second, velocity_second), False, 1)
    swap = [(0, 1), (1, 0)]
    other_sums = lax.ppermute(sums, "half", swap)
    inverse = lower_inverse(sums[:rank])
    other_inverse = lax.ppermute(inverse, "half", swap)
    basis = matmul_t(fresh, inverse)

    space_sums = jnp.where(on_space, sums, other_sums)
    velocity_sums = jnp.where(on_space, other_sums, sums)
    space_inverse = jnp.where(on_space, inverse, other_inverse)
    velocity_inverse = jnp.where(on_space, other_inverse, inverse)

    mixed = matmul(space_sums[rank : 2 * rank], coefficients)
    velocity_cross = velocity_sums[rank : 2 * rank]
    left = project(space_inverse, matmul(space_inverse, mixed))
    right = matmul(matmul_t(velocity_cross.T, velocity_inverse), velocity_inverse)
    middle = (1.0 - relax) * matmul_t(mixed, velocity_cross)
    middle = middle + relax * (space_sums[5 * rank][:, None] * velocity_sums[5 * rank][None, :])
    for k in range(3):
        rows = slice((2 + k) * rank, (3 + k) * rank)
        plus, minus = unpack_pair(velocity_sums[rows], velocity_sums[5 * rank + 1 + k])
        moment = space_sums[rows]
        middle = middle - time_step * matmul(matmul(moment, left), matmul(right, plus))
        middle = middle + time_step * matmul(project(moment, left), matmul(right, minus))
    block_rows = rank // lax.axis_size("half")
    own_inverse = lax.dynamic_slice_in_dim(
        space_inverse, lax.axis_index("half") * block_rows, block_rows, 0
    )
    return (basis[None], matmul_t(matmul(own_inverse, middle), velocity_inverse))


def solution(mesh):
    placed = (P("half", "rows", None), P(), P("rows"))
    return jax.shard_map(
        local,
        mesh=mesh,
        in_specs=placed,
        out_specs=(P("half", "rows", None), P("half", None)),
        check_vma=False,
    )
```

```python
import functools

import jax
import jax.numpy as jnp
from jax import lax
from jax.experimental import pallas as pl
from jax.experimental.pallas import tpu as pltpu
from jax.sharding import PartitionSpec as P

NY = 32
NZ = 32
VGRID = 64

time_step = 0.2
relax_time = 0.5
relax = time_step / relax_time

MESH = pl.DeviceIdType.MESH
PREC = lax.Precision.HIGHEST


def project(left, right):
    return lax.dot_general(
        left,
        right,
        (((0,), (0,)), ((), ())),
        precision=PREC,
        preferred_element_type=jnp.float32,
    )


def matmul(left, right):
    return jnp.dot(left, right, precision=PREC, preferred_element_type=jnp.float32)


def matmul_t(left, right):
    return lax.dot_general(
        left,
        right,
        (((1,), (1,)), ((), ())),
        precision=PREC,
        preferred_element_type=jnp.float32,
    )


def share_kernel(n, inner, swap, p_ref, o_ref, acc, got_in, got_out, mine, full, *sems):
    (s_a, r_a, s_b, r_b, s_s, r_s, s_c, r_c, s_d, r_d) = sems
    outer = n // inner
    half = lax.axis_index("half")
    row = lax.axis_index("rows")
    b = lax.rem(row, inner)
    a = row // inner
    q = p_ref.shape[0] // n
    w = q * outer

    def in_peer(k):
        return lax.rem(b + k, inner)

    def out_peer(k):
        return lax.rem(a + k, outer)

    peers = [(half, a * inner + in_peer(k)) for k in range(1, inner)]
    peers += [(half, out_peer(k) * inner + b) for k in range(1, outer)]
    if swap:
        peers.append((1 - half, row))
    barrier = pltpu.get_barrier_semaphore()
    for peer in peers:
        pl.semaphore_signal(barrier, inc=1, device_id=peer, device_id_type=MESH)
    pl.semaphore_wait(barrier, len(peers))

    def remote(src, dst, send, recv, peer):
        copy = pltpu.make_async_remote_copy(
            src_ref=src,
            dst_ref=dst,
            send_sem=send,
            recv_sem=recv,
            device_id=peer,
            device_id_type=MESH,
        )
        copy.start()
        return copy

    copies = []
    for k in range(1, inner):
        t = in_peer(k)
        rows = pl.ds(pl.multiple_of(t * w, 8), w)
        copies.append(
            remote(p_ref.at[rows], got_in.at[k - 1], s_a.at[k - 1], r_a.at[k - 1], (half, a * inner + t))
        )
    for copy in copies:
        copy.wait()
    total = p_ref[pl.ds(pl.multiple_of(b * w, 8), w), :]
    for k in range(1, inner):
        total = total + got_in[k - 1]
    acc[...] = total

    copies = []
    for k in range(1, outer):
        t = out_peer(k)
        rows = pl.ds(pl.multiple_of(t * q, 8), q)
        copies.append(
            remote(acc.at[rows], got_out.at[k - 1], s_b.at[k - 1], r_b.at[k - 1], (half, t * inner + b))
        )
    for copy in copies:
        copy.wait()
    piece = acc[pl.ds(pl.multiple_of(a * q, 8), q), :]
    for k in range(1, outer):
        piece = piece + got_out[k - 1]
    spot = pl.ds(pl.multiple_of(b * w + a * q, 8), q)
    if swap:
        mine[...] = piece
        copy = remote(mine, full.at[spot], s_s.at[0], r_s.at[0], (1 - half, row))
        copy.wait()
    else:
        full[spot, :] = piece

    copies = []
    for k in range(1, outer):
        t = out_peer(k)
        copies.append(
            remote(full.at[spot], full.at[spot], s_c.at[k - 1], r_c.at[k - 1], (half, t * inner + b))
        )
    for copy in copies:
        copy.wait()
    wide = pl.ds(pl.multiple_of(b * w, 8), w)
    copies = []
    for k in range(1, inner):
        t = in_peer(k)
        copies.append(
            remote(full.at[wide], full.at[wide], s_d.at[k - 1], r_d.at[k - 1], (half, a * inner + t))
        )
    for copy in copies:
        copy.wait()
    o_ref[...] = full[...]


def share_rows(payload, swap, collective_id):
    n = lax.axis_size("rows")
    inner = 4 if n % 4 == 0 and n > 4 else 2
    outer = n // inner
    rows, cols = payload.shape
    q = rows // n
    dma = pltpu.SemaphoreType.DMA
    sems = []
    for count in (inner - 1, outer - 1, 1, outer - 1, inner - 1):
        sems += [dma((count,)), dma((count,))]
    f32 = jnp.float32
    return pl.pallas_call(
        functools.partial(share_kernel, n, inner, swap),
        out_shape=jax.ShapeDtypeStruct((rows, cols), f32),
        in_specs=[pl.BlockSpec(memory_space=pltpu.VMEM)],
        out_specs=pl.BlockSpec(memory_space=pltpu.VMEM),
        scratch_shapes=[
            pltpu.VMEM((q * outer, cols), f32),
            pltpu.VMEM((inner - 1, q * outer, cols), f32),
            pltpu.VMEM((outer - 1, q, cols), f32),
            pltpu.VMEM((q, cols), f32),
            pltpu.VMEM((rows, cols), f32),
        ]
        + sems,
        compiler_params=pltpu.CompilerParams(
            collective_id=collective_id, has_side_effects=True, vmem_limit_bytes=32 * 1024 * 1024
        ),
    )(payload)


def padded_rows(rows, n):
    unit = 8 * n
    return (rows + unit - 1) // unit * unit


def velocity_grid(start, row_count, total_rows):
    last_points = total_rows // (VGRID * VGRID)
    row_index = start + jnp.arange(row_count, dtype=jnp.int32)
    third_index = row_index % last_points
    second = row_index // last_points % VGRID
    first_index = row_index // (last_points * VGRID)
    speeds = jnp.stack(
        [
            -1.0 + (2 * first_index + 1).astype(jnp.float32) / VGRID,
            -1.0 + (2 * second + 1).astype(jnp.float32) / VGRID,
            -1.0 + (2 * third_index + 1).astype(jnp.float32) / last_points,
        ]
    )
    maxwell = jnp.exp(-2.0 * jnp.sum(speeds * speeds, axis=0))
    return (speeds, maxwell)


def neighbour_plane(plane, step):
    count = lax.axis_size("rows")
    pairs = [(i, (i + step) % count) for i in range(count)]
    return lax.ppermute(plane, ("half", "rows"), pairs)


def back_slope(block, axis_index, low=None):
    if axis_index == 0:
        shifted = jnp.concatenate([low, block[:-1]], axis=0)
    else:
        shifted = jnp.roll(block, 1, axis_index)
    return (block - shifted).reshape(-1, block.shape[3])


def back_slopes(block, low):
    return [back_slope(block, axis_index, low) for axis_index in range(3)]


def front_slopes(block, high):
    width = block.shape[3]
    shifted = jnp.concatenate([block[1:], high], axis=0)
    slopes = [shifted - block]
    for axis_index in (1, 2):
        slopes.append(jnp.roll(block, -1, axis_index) - block)
    return [s.reshape(-1, width) for s in slopes]


def pack_payload(blocks, extras, rows, total_rows):
    rank = blocks[0].shape[1]
    used = sum(block.shape[0] for block in blocks)
    extra = jnp.stack(extras)
    pad = jnp.zeros((rows - used - extra.shape[0], rank), jnp.float32)
    return jnp.concatenate(blocks + [extra, pad]) * (1.0 / total_rows)


def triangle(rank):
    i = lax.broadcasted_iota(jnp.int32, (rank, rank), 0)
    j = lax.broadcasted_iota(jnp.int32, (rank, rank), 1)
    return i, j


def pack_pair(plus, minus):
    i, j = triangle(plus.shape[0])
    return jnp.where(i >= j, plus, minus), jnp.sum(jnp.where(i == j, minus, 0.0), axis=0)


def unpack_pair(packed, minus_diagonal):
    i, j = triangle(packed.shape[0])
    flipped = packed.T
    plus = jnp.where(i >= j, packed, flipped)
    minus = jnp.where(i < j, packed, jnp.where(i == j, minus_diagonal[None, :], flipped))
    return plus, minus


def velocity_blocks(factor, speeds):
    plus_speed = jnp.maximum(speeds, 0.0)
    minus_speed = jnp.minimum(speeds, 0.0)
    blocks, diagonals = [], []
    for k in range(3):
        block, diagonal = pack_pair(
            project(factor, plus_speed[k][:, None] * factor),
            project(factor, minus_speed[k][:, None] * factor),
        )
        blocks.append(block)
        diagonals.append(diagonal)
    return blocks, diagonals


def weighted(factor, weight):
    return project(weight[:, None], factor)[0]


def moments(factor, block, low, density, speeds, maxwell, on_space):
    rank = factor.shape[1]

    def space_part():
        blocks = [project(factor, back_slope(block, k)) for k in (1, 2)]
        zero_row = jnp.zeros((rank,), jnp.float32)
        blank = jnp.zeros((rank, rank), jnp.float32)
        return [blank] + blocks, [weighted(factor, density), zero_row, zero_row, zero_row]

    def velocity_part():
        blocks, diagonals = velocity_blocks(factor, speeds)
        return blocks, [weighted(factor, maxwell)] + diagonals

    blocks, extras = lax.cond(on_space, space_part, velocity_part)
    head = lax.cond(
        on_space, lambda: project(factor, back_slope(block, 0, low)), lambda: blocks[0]
    )
    return [head] + blocks[1:], extras


def inverse_kernel(g_ref, o_ref, work):
    rank = g_ref.shape[0]
    tile = 64
    lanes = 2 * tile
    work[:, :rank] = g_ref[...]
    i = lax.broadcasted_iota(jnp.int32, (rank, rank), 0)
    j = lax.broadcasted_iota(jnp.int32, (rank, rank), 1)
    work[:, rank:] = (i == j).astype(jnp.float32)
    row = lax.broadcasted_iota(jnp.int32, (tile, lanes), 0)
    lane = lax.broadcasted_iota(jnp.int32, (tile, lanes), 1)
    count = rank // tile
    for k in range(count):
        rows = slice(k * tile, (k + 1) * tile)
        base = k // 2 * lanes
        own = (k % 2) * tile
        other = tile - own
        in_own = (lane >= own) & (lane < own + tile)
        eye = (lane - other == row).astype(jnp.float32)
        m = jnp.where(in_own, work[rows, base : base + lanes], eye)
        for c in range(tile - 1):
            column = jnp.broadcast_to(m[:, own + c : own + c + 1], (tile, lanes))
            scaled = m[c : c + 1, :] / column[c : c + 1, :]
            m = m - jnp.where(row > c, column, 0.0) * scaled
        pivots = jnp.sum(jnp.where(lane - own == row, m, 0.0), axis=1, keepdims=True)
        small = (m * (1.0 / jnp.sqrt(pivots)))[:, other : other + tile]
        done = matmul(small, work[rows, :])
        o_ref[rows, :] = done[:, rank:]
        if k + 1 < count:
            top = (k + 1) // 2 * lanes
            upper = done[:, top:rank]
            at = lax.broadcasted_iota(jnp.int32, upper.shape, 1) + top
            upper = jnp.where(at >= (k + 1) * tile, upper, 0.0)
            update = project(upper, done[:, top : rank + base + lanes])
            work[top:, top : rank + base + lanes] -= update


def lower_inverse(gram):
    return pl.pallas_call(
        inverse_kernel,
        out_shape=jax.ShapeDtypeStruct(gram.shape, jnp.float32),
        in_specs=[pl.BlockSpec(memory_space=pltpu.VMEM)],
        out_specs=pl.BlockSpec(memory_space=pltpu.VMEM),
        scratch_shapes=[pltpu.VMEM((gram.shape[0], 2 * gram.shape[0]), jnp.float32)],
        compiler_params=pltpu.CompilerParams(vmem_limit_bytes=16 * 1024 * 1024),
        cost_estimate=pl.CostEstimate(flops=10**9, bytes_accessed=10**7, transcendentals=0),
    )(gram)


def local(factors, coefficients, density):
    rank = factors.shape[2]
    rows_here = factors.shape[1]
    n = lax.axis_size("rows")
    total_rows = rows_here * n
    planes = rows_here // (NY * NZ)
    start = lax.axis_index("rows") * rows_here
    on_space = lax.axis_index("half") == 0
    factor = factors[0]
    speeds, maxwell = velocity_grid(start, rows_here, total_rows)
    block = factor.reshape(planes, NY, NZ, rank)
    low = neighbour_plane(block[-1:], 1)
    first_plane, low = lax.optimization_barrier((block[:1], low))
    high = neighbour_plane(first_plane, -1)
    size_one = padded_rows(3 * rank + 4, n)

    payload = pack_payload(
        *moments(factor, block, low, density, speeds, maxwell, on_space), size_one, total_rows
    )
    other = share_rows(payload, True, 0)
    vector = other[3 * rank]

    def space_update():
        back = back_slopes(block, low)
        front = front_slopes(block, high)
        fresh = (1.0 - relax) * matmul(factor, coefficients)
        for k in range(3):
            plus, minus = unpack_pair(other[k * rank : (k + 1) * rank], other[3 * rank + 1 + k])
            fresh = fresh + matmul(back[k], matmul(coefficients * (-time_step), plus))
            fresh = fresh + matmul(front[k], matmul(coefficients * (-time_step), minus))
        return fresh + relax * (density[:, None] * vector[None, :])

    def velocity_update():
        plus_speed = jnp.maximum(speeds, 0.0) * (-time_step)
        minus_speed = jnp.minimum(speeds, 0.0) * time_step
        product = matmul_t(factor, coefficients)
        fresh = (1.0 - relax) * product
        for k in range(3):
            moment = other[k * rank : (k + 1) * rank]
            fresh = fresh + plus_speed[k][:, None] * matmul_t(product, moment)
            fresh = fresh + minus_speed[k][:, None] * matmul(product, moment)
        return fresh + relax * (maxwell[:, None] * vector[None, :])

    fresh = lax.cond(on_space, space_update, velocity_update)
    fresh_block = fresh.reshape(planes, NY, NZ, rank)
    fresh_low = neighbour_plane(fresh_block[-1:], 1)
    gram = project(fresh, fresh)
    cross = project(fresh, factor)

    size_two = padded_rows(5 * rank + 4, n)

    blocks, extras = moments(
        fresh, fresh_block, fresh_low, density, speeds, maxwell, on_space
    )
    payload = pack_payload([gram, cross] + blocks, extras, size_two, total_rows)
    sums = share_rows(payload, False, 1)
    swap = [(0, 1), (1, 0)]
    other_sums = lax.ppermute(sums, "half", swap)
    inverse = lower_inverse(sums[:rank])
    other_inverse = lax.ppermute(inverse, "half", swap)
    basis = matmul_t(fresh, inverse)

    space_sums = jnp.where(on_space, sums, other_sums)
    velocity_sums = jnp.where(on_space, other_sums, sums)
    space_inverse = jnp.where(on_space, inverse, other_inverse)
    velocity_inverse = jnp.where(on_space, other_inverse, inverse)

    mixed = matmul(space_sums[rank : 2 * rank], coefficients)
    velocity_cross = velocity_sums[rank : 2 * rank]
    left = project(space_inverse, matmul(space_inverse, mixed))
    right = matmul(matmul_t(velocity_cross.T, velocity_inverse), velocity_inverse)
    middle = (1.0 - relax) * matmul_t(mixed, velocity_cross)
    middle = middle + relax * (space_sums[5 * rank][:, None] * velocity_sums[5 * rank][None, :])
    for k in range(3):
        rows = slice((2 + k) * rank, (3 + k) * rank)
        plus, minus = unpack_pair(velocity_sums[rows], velocity_sums[5 * rank + 1 + k])
        moment = space_sums[rows]
        middle = middle - time_step * matmul(matmul(moment, left), matmul(right, plus))
        middle = middle + time_step * matmul(project(moment, left), matmul(right, minus))
    block_rows = rank // lax.axis_size("half")
    own_inverse = lax.dynamic_slice_in_dim(
        space_inverse, lax.axis_index("half") * block_rows, block_rows, 0
    )
    return (basis[None], matmul_t(matmul(own_inverse, middle), velocity_inverse))


def solution(mesh):
    placed = (P("half", "rows", None), P(), P("rows"))
    return jax.shard_map(
        local,
        mesh=mesh,
        in_specs=placed,
        out_specs=(P("half", "rows", None), P("half", None)),
        check_vma=False,
    )
```

```python
import functools

import jax
import jax.numpy as jnp
from jax import lax
from jax.experimental import pallas as pl
from jax.experimental.pallas import tpu as pltpu
from jax.sharding import PartitionSpec as P

NY = 32
NZ = 32
VGRID = 64

time_step = 0.2
relax_time = 0.5
relax = time_step / relax_time

MESH = pl.DeviceIdType.MESH
PREC = lax.Precision.HIGHEST


def project(left, right):
    return lax.dot_general(
        left,
        right,
        (((0,), (0,)), ((), ())),
        precision=PREC,
        preferred_element_type=jnp.float32,
    )


def matmul(left, right):
    return jnp.dot(left, right, precision=PREC, preferred_element_type=jnp.float32)


def matmul_t(left, right):
    return lax.dot_general(
        left,
        right,
        (((1,), (1,)), ((), ())),
        precision=PREC,
        preferred_element_type=jnp.float32,
    )


def share_kernel(n, inner, strips, swap, p_ref, o_ref, acc, got_in, got_out, mine, full, *sems):
    (s_a, r_a, s_b, r_b, s_s, r_s, s_c, r_c, s_d, r_d) = sems
    outer = n // inner
    half = lax.axis_index("half")
    row = lax.axis_index("rows")
    b = lax.rem(row, inner)
    a = row // inner
    q = p_ref.shape[0] // n
    w = q * outer

    def in_peer(k):
        return lax.rem(b + k, inner)

    def out_peer(k):
        return lax.rem(a + k, outer)

    peers = [(half, a * inner + in_peer(k)) for k in range(1, inner)]
    peers += [(half, out_peer(k) * inner + b) for k in range(1, outer)]
    if swap:
        peers.append((1 - half, row))
    barrier = pltpu.get_barrier_semaphore()
    for peer in peers:
        pl.semaphore_signal(barrier, inc=1, device_id=peer, device_id_type=MESH)
    pl.semaphore_wait(barrier, len(peers))

    def remote(src, dst, send, recv, peer):
        copy = pltpu.make_async_remote_copy(
            src_ref=src,
            dst_ref=dst,
            send_sem=send,
            recv_sem=recv,
            device_id=peer,
            device_id_type=MESH,
        )
        copy.start()
        return copy

    width = p_ref.shape[1] // strips
    strip = [slice(c * width, (c + 1) * width) for c in range(strips)]
    own = pl.ds(pl.multiple_of(b * w, 8), w)
    part = pl.ds(pl.multiple_of(a * q, 8), q)
    spot = pl.ds(pl.multiple_of(b * w + a * q, 8), q)
    fly = {}

    def start_a(c):
        fly[c] = []
        for k in range(1, inner):
            t = in_peer(k)
            rows = pl.ds(pl.multiple_of(t * w, 8), w)
            fly[c].append(
                remote(
                    p_ref.at[rows, strip[c]],
                    got_in.at[k - 1, :, strip[c]],
                    s_a.at[c, k - 1],
                    r_a.at[c, k - 1],
                    (half, a * inner + t),
                )
            )

    def start_b(c):
        total = p_ref[own, strip[c]]
        for k in range(1, inner):
            total = total + got_in[k - 1, :, strip[c]]
        acc[:, strip[c]] = total
        fly[c] = []
        for k in range(1, outer):
            t = out_peer(k)
            rows = pl.ds(pl.multiple_of(t * q, 8), q)
            fly[c].append(
                remote(
                    acc.at[rows, strip[c]],
                    got_out.at[k - 1, :, strip[c]],
                    s_b.at[c, k - 1],
                    r_b.at[c, k - 1],
                    (half, t * inner + b),
                )
            )

    def start_swap(c):
        piece = acc[part, strip[c]]
        for k in range(1, outer):
            piece = piece + got_out[k - 1, :, strip[c]]
        fly[c] = []
        if swap:
            mine[:, strip[c]] = piece
            fly[c].append(
                remote(
                    mine.at[:, strip[c]],
                    full.at[spot, strip[c]],
                    s_s.at[c],
                    r_s.at[c],
                    (1 - half, row),
                )
            )
        else:
            full[spot, strip[c]] = piece

    def start_c(c):
        fly[c] = []
        for k in range(1, outer):
            fly[c].append(
                remote(
                    full.at[spot, strip[c]],
                    full.at[spot, strip[c]],
                    s_c.at[c, k - 1],
                    r_c.at[c, k - 1],
                    (half, out_peer(k) * inner + b),
                )
            )

    def start_d(c):
        fly[c] = []
        for k in range(1, inner):
            fly[c].append(
                remote(
                    full.at[own, strip[c]],
                    full.at[own, strip[c]],
                    s_d.at[c, k - 1],
                    r_d.at[c, k - 1],
                    (half, a * inner + in_peer(k)),
                )
            )

    def land(c):
        for copy in fly[c]:
            copy.wait()

    for c in range(strips):
        start_a(c)
    for step in (start_b, start_swap, start_c, start_d):
        for c in range(strips):
            land(c)
            step(c)
    for c in range(strips):
        land(c)
    o_ref[...] = full[...]


def share_rows(payload, swap, collective_id):
    n = lax.axis_size("rows")
    inner = 4 if n % 4 == 0 and n > 4 else 2
    outer = n // inner
    rows, cols = payload.shape
    q = rows // n
    dma = pltpu.SemaphoreType.DMA
    sems = []
    strips = 2
    for count in (inner - 1, outer - 1, None, outer - 1, inner - 1):
        shape = (strips,) if count is None else (strips, count)
        sems += [dma(shape), dma(shape)]
    f32 = jnp.float32
    return pl.pallas_call(
        functools.partial(share_kernel, n, inner, strips, swap),
        out_shape=jax.ShapeDtypeStruct((rows, cols), f32),
        in_specs=[pl.BlockSpec(memory_space=pltpu.VMEM)],
        out_specs=pl.BlockSpec(memory_space=pltpu.VMEM),
        scratch_shapes=[
            pltpu.VMEM((q * outer, cols), f32),
            pltpu.VMEM((inner - 1, q * outer, cols), f32),
            pltpu.VMEM((outer - 1, q, cols), f32),
            pltpu.VMEM((q, cols), f32),
            pltpu.VMEM((rows, cols), f32),
        ]
        + sems,
        compiler_params=pltpu.CompilerParams(
            collective_id=collective_id, has_side_effects=True, vmem_limit_bytes=32 * 1024 * 1024
        ),
    )(payload)


def padded_rows(rows, n):
    unit = 8 * n
    return (rows + unit - 1) // unit * unit


def velocity_grid(start, row_count, total_rows):
    last_points = total_rows // (VGRID * VGRID)
    row_index = start + jnp.arange(row_count, dtype=jnp.int32)
    third_index = row_index % last_points
    second = row_index // last_points % VGRID
    first_index = row_index // (last_points * VGRID)
    speeds = jnp.stack(
        [
            -1.0 + (2 * first_index + 1).astype(jnp.float32) / VGRID,
            -1.0 + (2 * second + 1).astype(jnp.float32) / VGRID,
            -1.0 + (2 * third_index + 1).astype(jnp.float32) / last_points,
        ]
    )
    maxwell = jnp.exp(-2.0 * jnp.sum(speeds * speeds, axis=0))
    return (speeds, maxwell)


def neighbour_plane(plane, step):
    count = lax.axis_size("rows")
    pairs = [(i, (i + step) % count) for i in range(count)]
    return lax.ppermute(plane, ("half", "rows"), pairs)


def back_slope(block, axis_index, low=None):
    if axis_index == 0:
        shifted = jnp.concatenate([low, block[:-1]], axis=0)
    else:
        shifted = jnp.roll(block, 1, axis_index)
    return (block - shifted).reshape(-1, block.shape[3])


def back_slopes(block, low):
    return [back_slope(block, axis_index, low) for axis_index in range(3)]


def front_slopes(block, high):
    width = block.shape[3]
    shifted = jnp.concatenate([block[1:], high], axis=0)
    slopes = [shifted - block]
    for axis_index in (1, 2):
        slopes.append(jnp.roll(block, -1, axis_index) - block)
    return [s.reshape(-1, width) for s in slopes]


def pack_payload(blocks, extras, rows, total_rows):
    rank = blocks[0].shape[1]
    used = sum(block.shape[0] for block in blocks)
    extra = jnp.stack(extras)
    pad = jnp.zeros((rows - used - extra.shape[0], rank), jnp.float32)
    return jnp.concatenate(blocks + [extra, pad]) * (1.0 / total_rows)


def triangle(rank):
    i = lax.broadcasted_iota(jnp.int32, (rank, rank), 0)
    j = lax.broadcasted_iota(jnp.int32, (rank, rank), 1)
    return i, j


def pack_pair(plus, minus):
    i, j = triangle(plus.shape[0])
    return jnp.where(i >= j, plus, minus), jnp.sum(jnp.where(i == j, minus, 0.0), axis=0)


def unpack_pair(packed, minus_diagonal):
    i, j = triangle(packed.shape[0])
    flipped = packed.T
    plus = jnp.where(i >= j, packed, flipped)
    minus = jnp.where(i < j, packed, jnp.where(i == j, minus_diagonal, flipped))
    return plus, minus


def velocity_blocks(factor, speeds):
    plus_speed = jnp.maximum(speeds, 0.0)
    minus_speed = jnp.minimum(speeds, 0.0)
    blocks, diagonals = [], []
    for k in range(3):
        block, diagonal = pack_pair(
            project(factor, plus_speed[k][:, None] * factor),
            project(factor, minus_speed[k][:, None] * factor),
        )
        blocks.append(block)
        diagonals.append(diagonal)
    return blocks, diagonals


def weighted(factor, weight):
    return project(weight[:, None], factor)[0]


def moments(factor, block, low, density, speeds, maxwell, on_space):
    rank = factor.shape[1]

    def space_part():
        blocks = [project(factor, back_slope(block, k)) for k in (1, 2)]
        zero_row = jnp.zeros((rank,), jnp.float32)
        blank = jnp.zeros((rank, rank), jnp.float32)
        return [blank] + blocks, [weighted(factor, density), zero_row, zero_row, zero_row]

    def velocity_part():
        blocks, diagonals = velocity_blocks(factor, speeds)
        return blocks, [weighted(factor, maxwell)] + diagonals

    blocks, extras = lax.cond(on_space, space_part, velocity_part)
    head = lax.cond(
        on_space, lambda: project(factor, back_slope(block, 0, low)), lambda: blocks[0]
    )
    return [head] + blocks[1:], extras


def inverse_kernel(g_ref, o_ref, work):
    rank = g_ref.shape[0]
    tile = 64
    lanes = 2 * tile
    work[:, :rank] = g_ref[...]
    i = lax.broadcasted_iota(jnp.int32, (rank, rank), 0)
    j = lax.broadcasted_iota(jnp.int32, (rank, rank), 1)
    work[:, rank:] = (i == j).astype(jnp.float32)
    row = lax.broadcasted_iota(jnp.int32, (tile, lanes), 0)
    lane = lax.broadcasted_iota(jnp.int32, (tile, lanes), 1)
    count = rank // tile
    for k in range(count):
        rows = slice(k * tile, (k + 1) * tile)
        base = k // 2 * lanes
        own = (k % 2) * tile
        other = tile - own
        in_own = (lane >= own) & (lane < own + tile)
        eye = (lane - other == row).astype(jnp.float32)
        m = jnp.where(in_own, work[rows, base : base + lanes], eye)
        for c in range(tile - 1):
            column = jnp.broadcast_to(m[:, own + c : own + c + 1], (tile, lanes))
            scaled = m[c : c + 1, :] / column[c : c + 1, :]
            m = m - jnp.where(row > c, column, 0.0) * scaled
        pivots = jnp.sum(jnp.where(lane - own == row, m, 0.0), axis=1, keepdims=True)
        small = (m * (1.0 / jnp.sqrt(pivots)))[:, other : other + tile]
        done = matmul(small, work[rows, :])
        o_ref[rows, :] = done[:, rank:]
        if k + 1 < count:
            top = (k + 1) // 2 * lanes
            upper = done[:, top:rank]
            at = lax.broadcasted_iota(jnp.int32, upper.shape, 1) + top
            upper = jnp.where(at >= (k + 1) * tile, upper, 0.0)
            update = project(upper, done[:, top : rank + base + lanes])
            work[top:, top : rank + base + lanes] -= update


def lower_inverse(gram):
    return pl.pallas_call(
        inverse_kernel,
        out_shape=jax.ShapeDtypeStruct(gram.shape, jnp.float32),
        in_specs=[pl.BlockSpec(memory_space=pltpu.VMEM)],
        out_specs=pl.BlockSpec(memory_space=pltpu.VMEM),
        scratch_shapes=[pltpu.VMEM((gram.shape[0], 2 * gram.shape[0]), jnp.float32)],
        compiler_params=pltpu.CompilerParams(vmem_limit_bytes=16 * 1024 * 1024),
        cost_estimate=pl.CostEstimate(flops=10**9, bytes_accessed=10**7, transcendentals=0),
    )(gram)


def coefficient_kernel(first, space, velocity, space_inv, velocity_inv, coefficients, o_ref):
    rank = coefficients.shape[0]
    mixed = matmul(space[rank : 2 * rank], coefficients[...])
    cross = velocity[rank : 2 * rank]
    left = project(space_inv[...], matmul(space_inv[...], mixed))
    right = matmul(matmul_t(cross.T, velocity_inv[...]), velocity_inv[...])
    middle = (1.0 - relax) * matmul_t(mixed, cross)
    at = 5 * rank
    xb = jnp.broadcast_to(space[at : at + 1], (8, rank)).T[:, :1]
    middle = middle + (relax * xb) * velocity[at : at + 1]
    for k in range(3):
        rows = slice((2 + k) * rank, (3 + k) * rank)
        plus, minus = unpack_pair(velocity[rows], velocity[at + 1 + k : at + 2 + k])
        moment = space[rows]
        middle = middle - time_step * matmul(matmul(moment, left), matmul(right, plus))
        middle = middle + time_step * matmul(matmul(moment.T, left), matmul(right, minus))
    own = space_inv[first : first + o_ref.shape[0]]
    o_ref[...] = matmul_t(matmul(own, middle), velocity_inv[...])


def coefficient_rows(first, count, *operands):
    rank = operands[-1].shape[0]
    return pl.pallas_call(
        functools.partial(coefficient_kernel, first),
        out_shape=jax.ShapeDtypeStruct((count, rank), jnp.float32),
        in_specs=[pl.BlockSpec(memory_space=pltpu.VMEM)] * len(operands),
        out_specs=pl.BlockSpec(memory_space=pltpu.VMEM),
        compiler_params=pltpu.CompilerParams(vmem_limit_bytes=32 * 1024 * 1024),
    )(*operands)


def weight_kernel(moments, coefficients, o_ref):
    rank = coefficients.shape[0]
    scaled = coefficients[...] * (-time_step)
    for k in range(3):
        at = 3 * rank + 1 + k
        plus, minus = unpack_pair(moments[k * rank : (k + 1) * rank], moments[at : at + 1])
        o_ref[2 * k] = matmul(scaled, plus)
        o_ref[2 * k + 1] = matmul(scaled, minus)


def transport_weights(moments, coefficients):
    return pl.pallas_call(
        weight_kernel,
        out_shape=jax.ShapeDtypeStruct((6,) + coefficients.shape, jnp.float32),
        in_specs=[pl.BlockSpec(memory_space=pltpu.VMEM)] * 2,
        out_specs=pl.BlockSpec(memory_space=pltpu.VMEM),
        compiler_params=pltpu.CompilerParams(vmem_limit_bytes=16 * 1024 * 1024),
    )(moments, coefficients)


def local(factors, coefficients, density):
    rank = factors.shape[2]
    rows_here = factors.shape[1]
    n = lax.axis_size("rows")
    total_rows = rows_here * n
    planes = rows_here // (NY * NZ)
    start = lax.axis_index("rows") * rows_here
    on_space = lax.axis_index("half") == 0
    factor = factors[0]
    speeds, maxwell = velocity_grid(start, rows_here, total_rows)
    block = factor.reshape(planes, NY, NZ, rank)
    low = neighbour_plane(block[-1:], 1)
    first_plane, low = lax.optimization_barrier((block[:1], low))
    high = neighbour_plane(first_plane, -1)
    size_one = padded_rows(3 * rank + 4, n)

    payload = pack_payload(
        *moments(factor, block, low, density, speeds, maxwell, on_space), size_one, total_rows
    )
    other = share_rows(payload, True, 0)
    vector = other[3 * rank]

    def space_update():
        back = back_slopes(block, low)
        front = front_slopes(block, high)
        weights = transport_weights(other, coefficients)
        fresh = (1.0 - relax) * matmul(factor, coefficients)
        for k in range(3):
            fresh = fresh + matmul(back[k], weights[2 * k])
            fresh = fresh + matmul(front[k], weights[2 * k + 1])
        return fresh + relax * (density[:, None] * vector[None, :])

    def velocity_update():
        plus_speed = jnp.maximum(speeds, 0.0) * (-time_step)
        minus_speed = jnp.minimum(speeds, 0.0) * time_step
        product = matmul_t(factor, coefficients)
        fresh = (1.0 - relax) * product
        for k in range(3):
            moment = other[k * rank : (k + 1) * rank]
            fresh = fresh + plus_speed[k][:, None] * matmul_t(product, moment)
            fresh = fresh + minus_speed[k][:, None] * matmul(product, moment)
        return fresh + relax * (maxwell[:, None] * vector[None, :])

    fresh = lax.cond(on_space, space_update, velocity_update)
    fresh_block = fresh.reshape(planes, NY, NZ, rank)
    fresh_low = neighbour_plane(fresh_block[-1:], 1)
    gram = project(fresh, fresh)
    cross = project(fresh, factor)

    size_two = padded_rows(5 * rank + 4, n)

    blocks, extras = moments(
        fresh, fresh_block, fresh_low, density, speeds, maxwell, on_space
    )
    payload = pack_payload([gram, cross] + blocks, extras, size_two, total_rows)
    sums = share_rows(payload, False, 1)
    swap = [(0, 1), (1, 0)]
    other_sums = lax.ppermute(sums, "half", swap)
    inverse = lower_inverse(sums[:rank])
    other_inverse = lax.ppermute(inverse, "half", swap)
    basis = matmul_t(fresh, inverse)

    block_rows = rank // lax.axis_size("half")
    rows = lax.cond(
        on_space,
        lambda: coefficient_rows(
            0, block_rows, sums, other_sums, inverse, other_inverse, coefficients
        ),
        lambda: coefficient_rows(
            block_rows, block_rows, other_sums, sums, other_inverse, inverse, coefficients
        ),
    )
    return (basis[None], rows)


def solution(mesh):
    placed = (P("half", "rows", None), P(), P("rows"))
    return jax.shard_map(
        local,
        mesh=mesh,
        in_specs=placed,
        out_specs=(P("half", "rows", None), P("half", None)),
        check_vma=False,
    )
```

```python
import functools

import jax
import jax.numpy as jnp
from jax import lax
from jax.experimental import pallas as pl
from jax.experimental.pallas import tpu as pltpu
from jax.sharding import PartitionSpec as P

NY = 32
NZ = 32
VGRID = 64

time_step = 0.2
relax_time = 0.5
relax = time_step / relax_time

MESH = pl.DeviceIdType.MESH
PREC = lax.Precision.HIGHEST


def project(left, right):
    return lax.dot_general(
        left,
        right,
        (((0,), (0,)), ((), ())),
        precision=PREC,
        preferred_element_type=jnp.float32,
    )


def matmul(left, right):
    return jnp.dot(left, right, precision=PREC, preferred_element_type=jnp.float32)


def matmul_t(left, right):
    return lax.dot_general(
        left,
        right,
        (((1,), (1,)), ((), ())),
        precision=PREC,
        preferred_element_type=jnp.float32,
    )


def share_kernel(n, inner, strips, swap, p_ref, o_ref, acc, got_in, got_out, mine, full, *sems):
    (s_a, r_a, s_b, r_b, s_s, r_s, s_c, r_c, s_d, r_d) = sems
    outer = n // inner
    half = lax.axis_index("half")
    row = lax.axis_index("rows")
    b = lax.rem(row, inner)
    a = row // inner
    q = p_ref.shape[0] // n
    w = q * outer

    def in_peer(k):
        return lax.rem(b + k, inner)

    def out_peer(k):
        return lax.rem(a + k, outer)

    peers = [(half, a * inner + in_peer(k)) for k in range(1, inner)]
    peers += [(half, out_peer(k) * inner + b) for k in range(1, outer)]
    if swap:
        peers.append((1 - half, row))
    barrier = pltpu.get_barrier_semaphore()
    for peer in peers:
        pl.semaphore_signal(barrier, inc=1, device_id=peer, device_id_type=MESH)
    pl.semaphore_wait(barrier, len(peers))

    def remote(src, dst, send, recv, peer):
        copy = pltpu.make_async_remote_copy(
            src_ref=src,
            dst_ref=dst,
            send_sem=send,
            recv_sem=recv,
            device_id=peer,
            device_id_type=MESH,
        )
        copy.start()
        return copy

    width = p_ref.shape[1] // strips
    strip = [slice(c * width, (c + 1) * width) for c in range(strips)]
    own = pl.ds(pl.multiple_of(b * w, 8), w)
    part = pl.ds(pl.multiple_of(a * q, 8), q)
    spot = pl.ds(pl.multiple_of(b * w + a * q, 8), q)
    fly = {}

    def start_a(c):
        fly[c] = []
        for k in range(1, inner):
            t = in_peer(k)
            rows = pl.ds(pl.multiple_of(t * w, 8), w)
            fly[c].append(
                remote(
                    p_ref.at[rows, strip[c]],
                    got_in.at[k - 1, :, strip[c]],
                    s_a.at[c, k - 1],
                    r_a.at[c, k - 1],
                    (half, a * inner + t),
                )
            )

    def start_b(c):
        total = p_ref[own, strip[c]]
        for k in range(1, inner):
            total = total + got_in[k - 1, :, strip[c]]
        acc[:, strip[c]] = total
        fly[c] = []
        for k in range(1, outer):
            t = out_peer(k)
            rows = pl.ds(pl.multiple_of(t * q, 8), q)
            fly[c].append(
                remote(
                    acc.at[rows, strip[c]],
                    got_out.at[k - 1, :, strip[c]],
                    s_b.at[c, k - 1],
                    r_b.at[c, k - 1],
                    (half, t * inner + b),
                )
            )

    def start_swap(c):
        piece = acc[part, strip[c]]
        for k in range(1, outer):
            piece = piece + got_out[k - 1, :, strip[c]]
        fly[c] = []
        if swap:
            mine[:, strip[c]] = piece
            fly[c].append(
                remote(
                    mine.at[:, strip[c]],
                    full.at[spot, strip[c]],
                    s_s.at[c],
                    r_s.at[c],
                    (1 - half, row),
                )
            )
        else:
            full[spot, strip[c]] = piece

    def start_c(c):
        fly[c] = []
        for k in range(1, outer):
            fly[c].append(
                remote(
                    full.at[spot, strip[c]],
                    full.at[spot, strip[c]],
                    s_c.at[c, k - 1],
                    r_c.at[c, k - 1],
                    (half, out_peer(k) * inner + b),
                )
            )

    def start_d(c):
        fly[c] = []
        for k in range(1, inner):
            fly[c].append(
                remote(
                    full.at[own, strip[c]],
                    full.at[own, strip[c]],
                    s_d.at[c, k - 1],
                    r_d.at[c, k - 1],
                    (half, a * inner + in_peer(k)),
                )
            )

    def land(c):
        for copy in fly[c]:
            copy.wait()

    for c in range(strips):
        start_a(c)
    for step in (start_b, start_swap, start_c, start_d):
        for c in range(strips):
            land(c)
            step(c)
    for c in range(strips):
        land(c)
    o_ref[...] = full[...]


def share_rows(payload, swap, collective_id):
    n = lax.axis_size("rows")
    inner = 4 if n % 4 == 0 and n > 4 else 2
    outer = n // inner
    rows, cols = payload.shape
    q = rows // n
    dma = pltpu.SemaphoreType.DMA
    sems = []
    strips = 2
    for count in (inner - 1, outer - 1, None, outer - 1, inner - 1):
        shape = (strips,) if count is None else (strips, count)
        sems += [dma(shape), dma(shape)]
    f32 = jnp.float32
    return pl.pallas_call(
        functools.partial(share_kernel, n, inner, strips, swap),
        out_shape=jax.ShapeDtypeStruct((rows, cols), f32),
        in_specs=[pl.BlockSpec(memory_space=pltpu.VMEM)],
        out_specs=pl.BlockSpec(memory_space=pltpu.VMEM),
        scratch_shapes=[
            pltpu.VMEM((q * outer, cols), f32),
            pltpu.VMEM((inner - 1, q * outer, cols), f32),
            pltpu.VMEM((outer - 1, q, cols), f32),
            pltpu.VMEM((q, cols), f32),
            pltpu.VMEM((rows, cols), f32),
        ]
        + sems,
        compiler_params=pltpu.CompilerParams(
            collective_id=collective_id, has_side_effects=True, vmem_limit_bytes=32 * 1024 * 1024
        ),
    )(payload)


def padded_rows(rows, n):
    unit = 8 * n
    return (rows + unit - 1) // unit * unit


def velocity_grid(start, row_count, total_rows):
    last_points = total_rows // (VGRID * VGRID)
    row_index = start + jnp.arange(row_count, dtype=jnp.int32)
    third_index = row_index % last_points
    second = row_index // last_points % VGRID
    first_index = row_index // (last_points * VGRID)
    speeds = jnp.stack(
        [
            -1.0 + (2 * first_index + 1).astype(jnp.float32) / VGRID,
            -1.0 + (2 * second + 1).astype(jnp.float32) / VGRID,
            -1.0 + (2 * third_index + 1).astype(jnp.float32) / last_points,
        ]
    )
    maxwell = jnp.exp(-2.0 * jnp.sum(speeds * speeds, axis=0))
    return (speeds, maxwell)


def neighbour_plane(plane, step):
    count = lax.axis_size("rows")
    pairs = [(i, (i + step) % count) for i in range(count)]
    return lax.ppermute(plane, ("half", "rows"), pairs)


def back_slope(block, axis_index, low=None):
    if axis_index == 0:
        shifted = jnp.concatenate([low, block[:-1]], axis=0)
    else:
        shifted = jnp.roll(block, 1, axis_index)
    return (block - shifted).reshape(-1, block.shape[3])


def back_slopes(block, low):
    return [back_slope(block, axis_index, low) for axis_index in range(3)]


def front_slopes(block, high):
    width = block.shape[3]
    shifted = jnp.concatenate([block[1:], high], axis=0)
    slopes = [shifted - block]
    for axis_index in (1, 2):
        slopes.append(jnp.roll(block, -1, axis_index) - block)
    return [s.reshape(-1, width) for s in slopes]


def pack_payload(blocks, extras, rows, total_rows):
    rank = blocks[0].shape[1]
    used = sum(block.shape[0] for block in blocks)
    extra = jnp.stack(extras)
    pad = jnp.zeros((rows - used - extra.shape[0], rank), jnp.float32)
    return jnp.concatenate(blocks + [extra, pad]) * (1.0 / total_rows)


def triangle(rank):
    i = lax.broadcasted_iota(jnp.int32, (rank, rank), 0)
    j = lax.broadcasted_iota(jnp.int32, (rank, rank), 1)
    return i, j


def pack_pair(plus, minus):
    i, j = triangle(plus.shape[0])
    return jnp.where(i >= j, plus, minus), jnp.sum(jnp.where(i == j, minus, 0.0), axis=0)


def unpack_pair(packed, minus_diagonal):
    i, j = triangle(packed.shape[0])
    flipped = packed.T
    plus = jnp.where(i >= j, packed, flipped)
    minus = jnp.where(i < j, packed, jnp.where(i == j, minus_diagonal, flipped))
    return plus, minus


def velocity_blocks(factor, speeds):
    plus_speed = jnp.maximum(speeds, 0.0)
    minus_speed = jnp.minimum(speeds, 0.0)
    blocks, diagonals = [], []
    for k in range(3):
        block, diagonal = pack_pair(
            project(factor, plus_speed[k][:, None] * factor),
            project(factor, minus_speed[k][:, None] * factor),
        )
        blocks.append(block)
        diagonals.append(diagonal)
    return blocks, diagonals


def weighted(factor, weight):
    return project(weight[:, None], factor)[0]


def moments(factor, block, low, density, speeds, maxwell, on_space):
    rank = factor.shape[1]

    def space_part():
        blocks = [project(factor, back_slope(block, k)) for k in (1, 2)]
        zero_row = jnp.zeros((rank,), jnp.float32)
        blank = jnp.zeros((rank, rank), jnp.float32)
        return [blank] + blocks, [weighted(factor, density), zero_row, zero_row, zero_row]

    def velocity_part():
        blocks, diagonals = velocity_blocks(factor, speeds)
        return blocks, [weighted(factor, maxwell)] + diagonals

    blocks, extras = lax.cond(on_space, space_part, velocity_part)
    head = lax.cond(
        on_space, lambda: project(factor, back_slope(block, 0, low)), lambda: blocks[0]
    )
    return [head] + blocks[1:], extras


def inverse_kernel(g_ref, o_ref, work):
    rank = g_ref.shape[0]
    tile = 64
    lanes = 2 * tile
    work[:, :rank] = g_ref[...]
    i = lax.broadcasted_iota(jnp.int32, (rank, rank), 0)
    j = lax.broadcasted_iota(jnp.int32, (rank, rank), 1)
    work[:, rank:] = (i == j).astype(jnp.float32)
    row = lax.broadcasted_iota(jnp.int32, (tile, lanes), 0)
    lane = lax.broadcasted_iota(jnp.int32, (tile, lanes), 1)
    count = rank // tile
    for k in range(count):
        rows = slice(k * tile, (k + 1) * tile)
        base = k // 2 * lanes
        own = (k % 2) * tile
        other = tile - own
        in_own = (lane >= own) & (lane < own + tile)
        eye = (lane - other == row).astype(jnp.float32)
        m = jnp.where(in_own, work[rows, base : base + lanes], eye)
        for c in range(tile - 1):
            column = jnp.broadcast_to(m[:, own + c : own + c + 1], (tile, lanes))
            scaled = m[c : c + 1, :] / column[c : c + 1, :]
            m = m - jnp.where(row > c, column, 0.0) * scaled
        pivots = jnp.sum(jnp.where(lane - own == row, m, 0.0), axis=1, keepdims=True)
        small = (m * (1.0 / jnp.sqrt(pivots)))[:, other : other + tile]
        done = matmul(small, work[rows, :])
        o_ref[rows, :] = done[:, rank:]
        if k + 1 < count:
            top = (k + 1) // 2 * lanes
            upper = done[:, top:rank]
            at = lax.broadcasted_iota(jnp.int32, upper.shape, 1) + top
            upper = jnp.where(at >= (k + 1) * tile, upper, 0.0)
            update = project(upper, done[:, top : rank + base + lanes])
            work[top:, top : rank + base + lanes] -= update


def lower_inverse(gram):
    return pl.pallas_call(
        inverse_kernel,
        out_shape=jax.ShapeDtypeStruct(gram.shape, jnp.float32),
        in_specs=[pl.BlockSpec(memory_space=pltpu.VMEM)],
        out_specs=pl.BlockSpec(memory_space=pltpu.VMEM),
        scratch_shapes=[pltpu.VMEM((gram.shape[0], 2 * gram.shape[0]), jnp.float32)],
        compiler_params=pltpu.CompilerParams(vmem_limit_bytes=16 * 1024 * 1024),
        cost_estimate=pl.CostEstimate(flops=10**9, bytes_accessed=10**7, transcendentals=0),
    )(gram)


def coefficient_kernel(
    flag,
    sums,
    other_sums,
    inverse,
    other_inverse,
    coefficients,
    o_ref,
    space,
    velocity,
    space_inv,
    velocity_inv,
):
    @pl.when(flag[0] == 1)
    def _():
        space[...] = sums[...]
        velocity[...] = other_sums[...]
        space_inv[...] = inverse[...]
        velocity_inv[...] = other_inverse[...]

    @pl.when(flag[0] == 0)
    def _():
        space[...] = other_sums[...]
        velocity[...] = sums[...]
        space_inv[...] = other_inverse[...]
        velocity_inv[...] = inverse[...]

    rank = coefficients.shape[0]
    mixed = matmul(space[rank : 2 * rank], coefficients[...])
    cross = velocity[rank : 2 * rank]
    left = project(space_inv[...], matmul(space_inv[...], mixed))
    right = matmul(matmul_t(cross.T, velocity_inv[...]), velocity_inv[...])
    middle = (1.0 - relax) * matmul_t(mixed, cross)
    at = 5 * rank
    xb = jnp.broadcast_to(space[at : at + 1], (8, rank)).T[:, :1]
    middle = middle + (relax * xb) * velocity[at : at + 1]
    for k in range(3):
        rows = slice((2 + k) * rank, (3 + k) * rank)
        plus, minus = unpack_pair(velocity[rows], velocity[at + 1 + k : at + 2 + k])
        moment = space[rows]
        middle = middle - time_step * matmul(matmul(moment, left), matmul(right, plus))
        middle = middle + time_step * matmul(matmul(moment.T, left), matmul(right, minus))
    count = o_ref.shape[0]
    own = space_inv[pl.ds(pl.multiple_of((1 - flag[0]) * count, 8), count), :]
    o_ref[...] = matmul_t(matmul(own, middle), velocity_inv[...])


def coefficient_rows(count, flag, *operands):
    rank = operands[-1].shape[0]
    sums, inverse = operands[0].shape, operands[2].shape
    return pl.pallas_call(
        coefficient_kernel,
        out_shape=jax.ShapeDtypeStruct((count, rank), jnp.float32),
        in_specs=[pl.BlockSpec(memory_space=pltpu.SMEM)]
        + [pl.BlockSpec(memory_space=pltpu.VMEM)] * len(operands),
        out_specs=pl.BlockSpec(memory_space=pltpu.VMEM),
        scratch_shapes=[
            pltpu.VMEM(shape, jnp.float32) for shape in (sums, sums, inverse, inverse)
        ],
        compiler_params=pltpu.CompilerParams(vmem_limit_bytes=32 * 1024 * 1024),
    )(flag, *operands)


def weight_kernel(flag, moments, coefficients, o_ref):
    rank = coefficients.shape[0]

    @pl.when(flag[0] == 1)
    def _():
        scaled = coefficients[...] * (-time_step)
        for k in range(3):
            at = 3 * rank + 1 + k
            plus, minus = unpack_pair(moments[k * rank : (k + 1) * rank], moments[at : at + 1])
            o_ref[2 * k] = matmul(scaled, plus)
            o_ref[2 * k + 1] = matmul(scaled, minus)

    @pl.when(flag[0] == 0)
    def _():
        for k in range(3):
            moment = moments[k * rank : (k + 1) * rank]
            o_ref[2 * k] = moment.T * (-time_step)
            o_ref[2 * k + 1] = moment * time_step


def transport_weights(flag, moments, coefficients):
    return pl.pallas_call(
        weight_kernel,
        out_shape=jax.ShapeDtypeStruct((6,) + coefficients.shape, jnp.float32),
        in_specs=[pl.BlockSpec(memory_space=pltpu.SMEM)]
        + [pl.BlockSpec(memory_space=pltpu.VMEM)] * 2,
        out_specs=pl.BlockSpec(memory_space=pltpu.VMEM),
        compiler_params=pltpu.CompilerParams(vmem_limit_bytes=16 * 1024 * 1024),
    )(flag, moments, coefficients)


def local(factors, coefficients, density):
    rank = factors.shape[2]
    rows_here = factors.shape[1]
    n = lax.axis_size("rows")
    total_rows = rows_here * n
    planes = rows_here // (NY * NZ)
    start = lax.axis_index("rows") * rows_here
    on_space = lax.axis_index("half") == 0
    factor = factors[0]
    speeds, maxwell = velocity_grid(start, rows_here, total_rows)
    block = factor.reshape(planes, NY, NZ, rank)
    low = neighbour_plane(block[-1:], 1)
    size_one = padded_rows(3 * rank + 4, n)

    payload = pack_payload(
        *moments(factor, block, low, density, speeds, maxwell, on_space), size_one, total_rows
    )
    first_plane, payload = lax.optimization_barrier((block[:1], payload))
    high = neighbour_plane(first_plane, -1)
    other = share_rows(payload, True, 0)
    vector = other[3 * rank]

    flag = on_space.astype(jnp.int32).reshape(1)
    weights = transport_weights(flag, other, coefficients)
    product = matmul(factor, jnp.where(on_space, coefficients, coefficients.T))
    back = back_slopes(block, low)
    front = front_slopes(block, high)
    plus_speed = jnp.maximum(speeds, 0.0)
    minus_speed = jnp.minimum(speeds, 0.0)
    fresh = (1.0 - relax) * product
    for k in range(3):
        first = jnp.where(on_space, back[k], plus_speed[k][:, None] * product)
        second = jnp.where(on_space, front[k], minus_speed[k][:, None] * product)
        fresh = fresh + matmul(first, weights[2 * k])
        fresh = fresh + matmul(second, weights[2 * k + 1])
    source = jnp.where(on_space, density, maxwell)
    fresh = fresh + relax * (source[:, None] * vector[None, :])
    fresh_block = fresh.reshape(planes, NY, NZ, rank)
    fresh_low = neighbour_plane(fresh_block[-1:], 1)
    gram = project(fresh, fresh)
    cross = project(fresh, factor)

    size_two = padded_rows(5 * rank + 4, n)

    blocks, extras = moments(
        fresh, fresh_block, fresh_low, density, speeds, maxwell, on_space
    )
    payload = pack_payload([gram, cross] + blocks, extras, size_two, total_rows)
    sums = share_rows(payload, False, 1)
    swap = [(0, 1), (1, 0)]
    other_sums = lax.ppermute(sums, "half", swap)
    inverse = lower_inverse(sums[:rank])
    other_inverse = lax.ppermute(inverse, "half", swap)
    basis = matmul_t(fresh, inverse)

    block_rows = rank // lax.axis_size("half")
    rows = coefficient_rows(
        block_rows, flag, sums, other_sums, inverse, other_inverse, coefficients
    )
    return (basis[None], rows)


def solution(mesh):
    placed = (P("half", "rows", None), P(), P("rows"))
    return jax.shard_map(
        local,
        mesh=mesh,
        in_specs=placed,
        out_specs=(P("half", "rows", None), P("half", None)),
        check_vma=False,
    )
```
